32 devices in a mesh: groups: 2 (over x), node: 8 (over z, y), feat: 2 (over core).
Axes of the slice: x: 2, y: 2, z: 4, core: 2. Of those that a mesh axis runs over, the one named last changes fastest.
Arguments:
- features: bfloat16 [8192, 1024], P(('groups', 'node'), 'feat'), parts along dimension 0, may hold values from -6 to 6
- tile_list: int32 [32, 8], P('groups'), parts along dimension 0, may hold values from 0 to 15, as said below
- tile_values: bfloat16 [32, 8, 256, 256], P(('groups', 'node')), parts along dimension 0, may hold values from 0 to 1
- degree: int32 [8192], P(('groups', 'node')), parts along dimension 0, may hold values from 128 to 1024
- w_self: bfloat16 [1024, 1024], P('feat'), may hold values from -0.1875 to 0.1875
- w_neigh: bfloat16 [1024, 1024], P('feat'), may hold values from -3 to 3
- cotangent: bfloat16 [8192, 1024], P(('groups', 'node'), 'feat'), parts along dimension 0, may hold values from -6 to 6
Outputs:
- hidden: bfloat16 [8192, 1024], P(('groups', 'node'), 'feat'), parts along dimension 0
- grad_features: bfloat16 [8192, 1024], P(('groups', 'node'), 'feat'), parts along dimension 0
- grad_self: float32 [2048, 1024], P(('groups', 'feat'), 'node'), parts along dimension 0
- grad_neigh: float32 [2048, 1024], P(('groups', 'feat'), 'node'), parts along dimension 0
The draws below stay inside these ranges and needn't reach their ends.
There are 2 independent parts, one for each index of `groups`. The reference program is written for one: setup_inputs(seed, part) draws one part's arguments, and reference() takes and returns one part's arrays. A program takes and returns all parts, laid end to end along the dimension named above; an argument that names none is the same for every part. Nothing has to cross between parts.
Inputs may be any that keep to these rules, and one draw needn't show every extreme that they name: `tile_list`: the 16 entries of one node device's 2 block rows name at most one block of each other node device, and blocks of exactly min(14, 7) other node devices; every other entry names one of the device's own blocks.
All inputs are finite; a program needn't handle non-finite values.
Results may differ from the reference program's by a relative error of at most 0.008.
Values may be sent and summed in bfloat16 or wider, within the bound.
No kernel may reach another device: no remote copies, remote signals or barrier semaphores. Data moves between devices by JAX's collectives and lax.ppermute only.
A program may use at most 128 MiB of HBM per device.

```python
import jax
import jax.numpy as jnp
from jax import lax

D = 1024
H = 1024
TILE = 256
TPR = 8
BLK_DEV = 2
NBLK = 16
NODES = 4096


def draw_tile_list(key, part):
    key = jax.random.fold_in(key, 7)
    node_count = NBLK // BLK_DEV
    slot_count = BLK_DEV * TPR
    remote_count = min(BLK_DEV * (TPR - 1), node_count - 1)
    subkeys = jax.random.split(key, 5)
    hotness = jax.random.randint(subkeys[0], (node_count,), 0, 4) * 4
    noise_part = jax.random.randint(subkeys[1], (node_count, node_count), 0, 8)
    columns = jnp.arange(node_count, dtype=jnp.int32)
    scores = (noise_part + hotness[None, :]) * node_count + columns[None, :]
    scores = jnp.where(columns[:, None] == columns[None, :], -1, scores)
    ignored_values, sources = lax.top_k(scores, remote_count)
    chosen_block = jax.random.randint(subkeys[2], (node_count, remote_count), 0, BLK_DEV)
    remote_slots = sources.astype(jnp.int32) * BLK_DEV + chosen_block
    own_slots = jax.random.randint(subkeys[3], (node_count, slot_count - remote_count), 0, BLK_DEV) + columns[:, None] * BLK_DEV
    chosen = jnp.concatenate([remote_slots, own_slots], axis=1)
    order_keys = jax.random.randint(subkeys[4], (node_count, slot_count), 0, 1 << 20) * slot_count + jnp.arange(slot_count, dtype=jnp.int32)[None, :]
    ordering = jnp.argsort(order_keys, axis=1)
    shuffled = jnp.take_along_axis(chosen, ordering, axis=1)
    return shuffled.reshape(NBLK, TPR).astype(jnp.int32)


def place_ends(entries, stream_key, least, largest):
    extent = entries.shape
    place = [jax.random.randint(jax.random.fold_in(stream_key, axis), (), 0, extent[axis]) for axis in range(len(extent))]
    entries = entries.at[tuple(place)].set(least)
    longest = extent.index(max(extent))
    place[longest] = (place[longest] + 1) % extent[longest]
    return entries.at[tuple(place)].set(largest)


def with_spikes(values, stream_key, source, target, blocks, factor):
    owner, partner = [(jnp.arange(values.shape[axis_at]) // (values.shape[axis_at] // blocks)).reshape([-1 if axis == axis_at else 1 for axis in range(values.ndim)]) for axis_at in (source, target)]
    chosen = jax.random.permutation(stream_key, blocks)[partner]
    strong = (owner == chosen) | (owner == (partner + blocks // 2) % blocks)
    return jnp.where(strong, factor * values, values)


def levels(own_key, extent, cuts, smallest, high):
    def one(axis_at, blocks):
        heights = jax.random.uniform(jax.random.fold_in(jax.random.fold_in(own_key, 6), axis_at), (blocks,), jnp.float32, smallest / len(cuts), high / len(cuts))
        return jnp.repeat(jnp.exp(heights), extent[axis_at] // blocks).reshape((-1,) + (1,) * (len(extent) - axis_at - 1))

    loudness = one(*cuts[0])
    for cut in cuts[1:]:
        loudness = loudness * one(*cut)
    return loudness


def gaussian(own_key, dims, scale, most, cuts=(), held_as=jnp.bfloat16):
    array = scale * jax.random.normal(own_key, dims, jnp.float32)
    if cuts:
        array = array * levels(own_key, dims, cuts, -0.22, 0.18)
    return jnp.clip(array, -most, most).astype(held_as)


def bell_draw_with(key, extent, scale, limit, cuts, heavy, kind=jnp.bfloat16):
    entries = scale * jax.random.normal(key, extent, jnp.float32)
    if cuts:
        entries = entries * levels(key, extent, cuts, -0.22, 0.18)
    return jnp.clip(with_spikes(entries, jax.random.fold_in(key, 3), *heavy), -limit, limit).astype(kind)


def setup_inputs(seed: int = 0, part: int = 0) -> dict:
    seeds = jax.random.split(jax.random.key(seed), 8)
    part_keys = jax.random.split(jax.random.fold_in(seeds[7], part), 8)
    features = gaussian(part_keys[0], (NODES, D), 1.0, 6.0, ((0, 8), (1, 2)))
    tile_list = draw_tile_list(jax.random.fold_in(jax.random.fold_in(seeds[7], part), 71), part)
    tile_values = jnp.clip(1.0 * jax.random.uniform(part_keys[2], (NBLK, TPR, TILE, TILE), jnp.float32) ** levels(part_keys[2], (NBLK, TPR, TILE, TILE), ((0, 8),), -0.2, 0.2), 0.0, 1.0).astype(jnp.bfloat16)
    degree = place_ends(jax.random.randint(part_keys[3], (NODES,), TPR * TILE // 16, TPR * TILE // 2 + 1), jax.random.fold_in(part_keys[3], 1), TPR * TILE // 16, (TPR * TILE // 2 + 1) - 1).astype(jnp.int32)
    w_self = gaussian(seeds[4], (D, H), D ** -0.5, 0.1875, ((0, 2),))
    w_neigh = gaussian(seeds[5], (D, H), (max(D // 256, 1)) ** -0.5, 3.0, ((0, 2),))
    cotangent = bell_draw_with(part_keys[6], (NODES, H), 1.0, 6.0, ((0, 8), (1, 2)), (0, 1, 8, 2.0))
    return dict(features=features, tile_list=tile_list, tile_values=tile_values, degree=degree, w_self=w_self, w_neigh=w_neigh, cotangent=cotangent)


def reference(features, tile_list, tile_values, degree, w_self, w_neigh, cotangent):
    block_total = tile_list.shape[0]
    feature_width = features.shape[1]
    node_count = block_total // BLK_DEV
    slot_count = BLK_DEV * TPR
    blocks = features.reshape(block_total, TILE, feature_width)
    inverse = (1.0 / degree.astype(jnp.float32)).reshape(block_total, TILE, 1)

    def aggregate_row(inputs):
        values, columns, inverse_row = inputs
        picked = blocks[columns].astype(jnp.float32)
        summed = jnp.einsum("tij,tjf->if", values.astype(jnp.float32), picked)
        return (summed * inverse_row).astype(jnp.bfloat16)

    aggregated = lax.map(aggregate_row, (tile_values, tile_list, inverse)).reshape(-1, feature_width)
    pre_act = jnp.dot(features, w_self, preferred_element_type=jnp.float32) + jnp.dot(aggregated, w_neigh, preferred_element_type=jnp.float32)
    sigmoid_z = jax.nn.sigmoid(pre_act)
    hidden = (pre_act * sigmoid_z).astype(jnp.bfloat16)
    slope = (cotangent.astype(jnp.float32) * sigmoid_z * (1.0 + pre_act * (1.0 - sigmoid_z))).astype(jnp.bfloat16)
    grad_self = jnp.dot(features.T, slope, preferred_element_type=jnp.float32)
    grad_neigh = jnp.dot(aggregated.T, slope, preferred_element_type=jnp.float32)
    back_self = jnp.dot(slope, w_self.T, preferred_element_type=jnp.float32)
    back_neigh = jnp.dot(slope, w_neigh.T, preferred_element_type=jnp.float32)
    scaled = (back_neigh.reshape(block_total, TILE, feature_width) * inverse).astype(jnp.bfloat16)
    block_ids = jnp.arange(block_total, dtype=jnp.int32)

    def spread_device(carry, device):
        start = (device * BLK_DEV).astype(jnp.int32)
        values = lax.dynamic_slice_in_dim(tile_values, start, BLK_DEV, 0).astype(jnp.float32)
        columns = lax.dynamic_slice_in_dim(tile_list, start, BLK_DEV, 0).reshape(slot_count)
        rows_in = lax.dynamic_slice_in_dim(scaled, start, BLK_DEV, 0).astype(jnp.float32)
        pieces = jnp.einsum("btij,bif->btjf", values, rows_in).reshape(slot_count, TILE, feature_width)
        inside = (columns // BLK_DEV) == device
        matching = columns[None, :] == block_ids[:, None]
        remote_hot = (matching & ~inside[None, :]).astype(jnp.float32)
        local_hot = (matching & inside[None, :]).astype(jnp.float32)
        remote_sum = jnp.einsum("cs,srf->crf", remote_hot, pieces).astype(jnp.bfloat16)
        remote_sum = lax.optimization_barrier(remote_sum).astype(jnp.float32)
        local_sum = jnp.einsum("cs,srf->crf", local_hot, pieces)
        return carry + remote_sum + local_sum, None

    starting = jnp.zeros((block_total, TILE, feature_width), jnp.float32)
    spread, ignored_values = lax.scan(spread_device, starting, jnp.arange(node_count, dtype=jnp.int32))
    grad_features = (back_self + spread.reshape(-1, feature_width)).astype(jnp.bfloat16)
    return (hidden, grad_features, grad_self, grad_neigh)
```

```python
import functools

import jax
import jax.numpy as jnp
from jax import lax
from jax.experimental import pallas as pl
from jax.experimental.pallas import tpu as pltpu
from jax.sharding import PartitionSpec as P

TILE = 256
TPR = 8
BF16, F32 = jnp.bfloat16, jnp.float32
SMEM = pl.BlockSpec(memory_space=pltpu.SMEM)
VMEM = pl.BlockSpec(memory_space=pltpu.VMEM)
ROWS_BY_COLS = (((1,), (0,)), ((), ()))
COLS_BY_COLS = (((1,), (1,)), ((), ()))


def mul(a, b, dims=ROWS_BY_COLS):
    return lax.dot_general(a, b, dims, preferred_element_type=F32)


def block(index):
    return pl.ds(pl.multiple_of(index * TILE, TILE), TILE)


def local_call(kernel, outs, ins, flops, scratch=(), scalars=1):
    moved = sum(a.size * a.dtype.itemsize for a in ins)
    moved += sum(o.size * o.dtype.itemsize for o in outs)
    return pl.pallas_call(
        kernel,
        out_shape=outs,
        in_specs=[SMEM] * scalars + [VMEM] * (len(ins) - scalars),
        out_specs=[VMEM] * len(outs),
        scratch_shapes=list(scratch),
        compiler_params=pltpu.CompilerParams(vmem_limit_bytes=44 * 1024 * 1024),
        cost_estimate=pl.CostEstimate(flops=flops, bytes_accessed=moved, transcendentals=0),
    )(*ins)


def combine(code, tiles, first, count):
    own_blocks = tiles.shape[0]
    rows = own_blocks * TILE

    def kernel(code_ref, tiles_ref, out_ref, flipped_ref, total):
        source = pl.program_id(0) + first
        for r in range(own_blocks):
            total[...] = jnp.zeros_like(total)
            for t in range(TPR):

                @pl.when(code_ref[r * TPR + t] == source)
                def _():
                    total[...] += tiles_ref[r, t].astype(F32)

            whole = total[...]
            out_ref[0, r * TILE : (r + 1) * TILE, :] = whole.astype(BF16)
            flipped_ref[0, :, r * TILE : (r + 1) * TILE] = whole.T.astype(BF16)

    return pl.pallas_call(
        kernel,
        grid=(count,),
        out_shape=[
            jax.ShapeDtypeStruct((count, rows, TILE), BF16),
            jax.ShapeDtypeStruct((count, TILE, rows), BF16),
        ],
        in_specs=[SMEM, pl.BlockSpec(tiles.shape, lambda j: (0, 0, 0, 0))],
        out_specs=[
            pl.BlockSpec((1, rows, TILE), lambda j: (j, 0, 0)),
            pl.BlockSpec((1, TILE, rows), lambda j: (j, 0, 0)),
        ],
        scratch_shapes=[pltpu.VMEM((TILE, TILE), F32)],
        compiler_params=pltpu.CompilerParams(vmem_limit_bytes=32 * 1024 * 1024),
        cost_estimate=pl.CostEstimate(
            flops=0, bytes_accessed=2 * tiles.size + 4 * count * rows * TILE, transcendentals=0
        ),
    )(code, tiles)


def early_kernel(info, matrix, own, partner, *rest):
    *direct, out = rest
    count = len(direct)
    total = mul(matrix[0], own[:TILE]) + mul(matrix[1], own[TILE:])
    for k in range(count):
        total += mul(matrix[2 + k], direct[k][...])
    out[...] = total + mul(matrix[2 + count], partner[block(info[2, count + 1]), :])


def late_kernel(info, matrix, early, inverse, *rest):
    *passed, out, away = rest
    total = early[...]
    for k, piece in enumerate(passed):
        total += mul(matrix[k], piece[...])
    out[...] = (total * inverse[...]).astype(BF16)
    away[...] = out[block(1 - info[3, 0]), :]


def slope_kernel(info, self_part, agg, agg_in, w_own, w_other, cot_own, cot_in, slope, keep, away, cot, hid):
    feat = info[3, 0]
    width = cot_own.shape[1]
    mine = pl.ds(pl.multiple_of(feat * width, width), width)
    other = pl.ds(pl.multiple_of((1 - feat) * width, width), width)
    cot[:, mine] = cot_own[...]
    cot[:, other] = cot_in[...]
    own_rows = agg[block(feat), :]
    step = 256
    for c in range(0, slope.shape[1], step):
        cols = slice(c, c + step)
        pre = self_part[:, cols] + mul(own_rows, w_own[:, cols]) + mul(agg_in[...], w_other[:, cols])
        s = jax.nn.sigmoid(pre)
        hid[:, cols] = (pre * s).astype(BF16)
        slope[:, cols] = (cot[:, cols].astype(F32) * s * (1.0 + pre * (1.0 - s))).astype(BF16)
    keep[...] = hid[:, mine]
    away[...] = hid[:, other]


def pieces_kernel(count, info, slope_own, slope_in, w_neigh, inverse, early, late, slope, scaled, partner, *outs):
    feat = info[3, 0]
    slope[block(feat), :] = slope_own[...]
    slope[block(1 - feat), :] = slope_in[...]
    scaled[...] = (mul(slope[...], w_neigh[...], COLS_BY_COLS) * inverse[...]).astype(BF16)
    for k in range(count):
        outs[k][...] = mul(late[k], scaled[...]).astype(BF16)
    for k in range(count):
        outs[count + k][...] = mul(early[2 + k], scaled[...]).astype(BF16)
    partner[...] = mul(early[2 + count], scaled[...])


def terms_kernel(info, slope, features_t, agg_t, keep, away):
    node = info[3, 1]
    low = node % 2
    high = node // 2
    width = keep.shape[3]
    for which, left in enumerate((features_t, agg_t)):
        for p in range(keep.shape[0]):
            both = mul(left[...], slope[:, 2 * p * width : 2 * (p + 1) * width])
            a, b = both[:, :width], both[:, width:]
            at = jnp.bitwise_xor(high, p)
            keep[at, which] = jnp.where(low == 0, a, b)
            away[at, which] = jnp.where(low == 0, b, a).astype(BF16)


def base_kernel(info, slope, w_self, scaled, early, out):
    back = mul(slope[...], w_self[...], COLS_BY_COLS)
    for b in range(2):
        rows = slice(b * TILE, (b + 1) * TILE)
        out[rows, :] = back[rows] + mul(early[b], scaled[...])


def partner_kernel(info, own, *rest):
    *passed, out, total = rest
    total[...] = jnp.zeros_like(total)
    total[block(info[2, len(passed) + 1]), :] = own[...]
    for k, piece in enumerate(passed):
        total[block(info[1, k + 1]), :] += piece[...].astype(F32)
    out[...] = total[...].astype(BF16)


def final_kernel(info, base, partner, *rest):
    *direct, out, total = rest
    total[...] = base[...] + partner[...].astype(F32)
    for k, piece in enumerate(direct):
        total[block(info[0, k + 1]), :] += piece[...].astype(F32)
    out[...] = total[...].astype(BF16)


def on_device(features, tile_list, tile_values, degree, w_self, w_neigh, cotangent):
    nodes = lax.axis_size("node")
    me = lax.axis_index("node")
    feat = lax.axis_index("feat")
    own_rows, width = features.shape
    hidden_width = w_self.shape[1]
    own_blocks = own_rows // TILE
    slots = own_blocks * TPR
    across = nodes // 2
    near = range(1, across)

    def swap(x):
        return lax.ppermute(x, "feat", [(0, 1), (1, 0)])

    def hop(x, k):
        return lax.ppermute(x, "node", [(i, i ^ k) for i in range(nodes)])

    def halves(x):
        a, b = x[:TILE], x[TILE:]
        first = feat == 0
        return jnp.where(first, a, b), jnp.where(first, b, a)

    shape = jax.ShapeDtypeStruct

    ids = jnp.arange(nodes, dtype=jnp.int32)
    everyone = tile_list.reshape(1, nodes, slots)
    at = (ids ^ me)[:, None, None]
    that = ids[None, :, None] == at
    this = ids[None, :, None] == me
    far = me ^ across
    def seen(mask):
        return jnp.any(mask, axis=(1, 2)).astype(jnp.int32)
    info = jnp.stack(
        [
            seen(that & (everyone == 2 * me + 1)),
            seen(that & (everyone == 2 * far + 1)),
            seen(this & (everyone == 2 * at + 1)),
            jnp.where(ids == 0, feat, me).astype(jnp.int32),
        ]
    )

    partner = hop(features, across)
    direct = [hop(lax.dynamic_slice_in_dim(features, info[0, k] * TILE, TILE, 0), k) for k in near]

    mine = lax.dynamic_slice_in_dim(tile_list, me * own_blocks, own_blocks, 0).reshape(slots)
    owner = mine // own_blocks
    code = jnp.where(owner == me, mine % own_blocks, 1 + (owner ^ me))
    early, early_t = combine(code, tile_values, 0, across + 2)
    late, late_t = combine(code, tile_values, across + 2, across - 1)
    inverse = (1.0 / degree.astype(F32)).reshape(own_rows, 1)

    rows_own, rows_away = halves(features)
    cot_own, cot_away = halves(cotangent)
    rows_in, cot_in = swap(rows_away), swap(cot_away)
    w_self_in, w_neigh_in = swap(w_self), swap(w_neigh)
    self_part = mul(rows_own, w_self) + mul(rows_in, w_self_in)
    features_t = features.T

    passed = [hop(lax.dynamic_slice_in_dim(partner, info[1, k] * TILE, TILE, 0), k) for k in near]
    tile_flops = 2 * own_rows * TILE * width
    (summed,) = local_call(
        early_kernel,
        [shape((own_rows, width), F32)],
        [info, early, features, partner, *direct],
        (across + 2) * tile_flops,
    )
    agg, agg_away = local_call(
        late_kernel,
        [shape((own_rows, width), BF16), shape((TILE, width), BF16)],
        [info, late, summed, inverse, *passed],
        across * tile_flops,
    )
    agg_in = swap(agg_away)
    agg_t = agg.T
    slope_own, hid_keep, hid_away = local_call(
        slope_kernel,
        [shape((TILE, hidden_width), BF16), shape((TILE, width), BF16), shape((TILE, width), BF16)],
        [info, self_part, agg, agg_in, w_neigh, w_neigh_in, cot_own, cot_in],
        4 * TILE * width * hidden_width,
        [pltpu.VMEM((TILE, hidden_width), BF16)] * 2,
    )
    slope_in = swap(slope_own)
    hid_in = swap(hid_away)
    hidden = jnp.where(feat == 0, jnp.concatenate([hid_keep, hid_in]), jnp.concatenate([hid_in, hid_keep]))

    count = across - 1
    piece = shape((TILE, width), BF16)
    slope, scaled, own_piece, *pieces = local_call(
        functools.partial(pieces_kernel, count),
        [shape((own_rows, hidden_width), BF16), shape((own_rows, width), BF16), shape((TILE, width), F32)]
        + [piece] * (2 * count),
        [info, slope_own, slope_in, w_neigh, inverse, early_t, late_t],
        2 * own_rows * hidden_width * width + (nodes - 1) * tile_flops,
    )
    back_passed = [hop(pieces[k - 1], k) for k in near]
    back_direct = [hop(pieces[count + k - 1], k) for k in near]

    columns = hidden_width // nodes
    if columns % 128 == 0:
        groups = nodes // 2
        keep, away = local_call(
            terms_kernel,
            [shape((groups, 2, width, columns), F32), shape((groups, 2, width, columns), BF16)],
            [info, slope, features_t, agg_t],
            4 * own_rows * width * hidden_width,
        )
        bit = 1
        while True:
            keep = keep + hop(away, bit).astype(F32)
            bit *= 2
            if bit == nodes:
                break
            keep, away = keep[0::2], keep[1::2].astype(BF16)
        grad_self, grad_neigh = keep[0, 0], keep[0, 1]
    else:
        grad_self, grad_neigh = (
            lax.psum_scatter(mul(left, slope), "node", scatter_dimension=1, tiled=True)
            for left in (features_t, agg_t)
        )

    (base,) = local_call(
        base_kernel,
        [shape((own_rows, width), F32)],
        [info, slope, w_self, scaled, early_t],
        2 * own_rows * hidden_width * width + 2 * tile_flops,
    )
    (to_partner,) = local_call(
        partner_kernel,
        [shape((own_rows, width), BF16)],
        [info, own_piece, *back_passed],
        0,
        [pltpu.VMEM((own_rows, width), F32)],
    )
    from_partner = hop(to_partner, across)
    (grad_features,) = local_call(
        final_kernel,
        [shape((own_rows, width), BF16)],
        [info, base, from_partner, *back_direct],
        0,
        [pltpu.VMEM((own_rows, width), F32)],
    )
    return (hidden, grad_features, grad_self, grad_neigh)


def solution(mesh):
    return jax.shard_map(
        on_device,
        mesh=mesh,
        in_specs=(
            P(("groups", "node"), "feat"),
            P("groups", None),
            P(("groups", "node"), None, None, None),
            P(("groups", "node")),
            P("feat", None),
            P("feat", None),
            P(("groups", "node"), "feat"),
        ),
        out_specs=(
            P(("groups", "node"), "feat"),
            P(("groups", "node"), "feat"),
            P(("groups", "feat"), "node"),
            P(("groups", "feat"), "node"),
        ),
        check_vma=False,
    )
```

```python
import functools

import jax
import jax.numpy as jnp
from jax import lax
from jax.experimental import pallas as pl
from jax.experimental.pallas import tpu as pltpu
from jax.sharding import PartitionSpec as P

TILE = 256
TPR = 8
BF16, F32 = jnp.bfloat16, jnp.float32
SMEM = pl.BlockSpec(memory_space=pltpu.SMEM)
VMEM = pl.BlockSpec(memory_space=pltpu.VMEM)
ROWS_BY_COLS = (((1,), (0,)), ((), ()))
COLS_BY_COLS = (((1,), (1,)), ((), ()))


def mul(a, b, dims=ROWS_BY_COLS):
    return lax.dot_general(a, b, dims, preferred_element_type=F32)


def block(index):
    return pl.ds(pl.multiple_of(index * TILE, TILE), TILE)


def after(x, *earlier):
    return lax.optimization_barrier((x, earlier))[0]


def local_call(kernel, outs, ins, flops, scratch=(), scalars=1):
    moved = sum(a.size * a.dtype.itemsize for a in ins)
    moved += sum(o.size * o.dtype.itemsize for o in outs)
    held = moved + 8 * 1024 * 1024
    return pl.pallas_call(
        kernel,
        out_shape=outs,
        in_specs=[SMEM] * scalars + [VMEM] * (len(ins) - scalars),
        out_specs=[VMEM] * len(outs),
        scratch_shapes=list(scratch),
        compiler_params=pltpu.CompilerParams(vmem_limit_bytes=held),
        cost_estimate=pl.CostEstimate(flops=flops, bytes_accessed=moved, transcendentals=0),
    )(*ins)


def combine(code, tiles, first, count):
    own_blocks = tiles.shape[0]
    rows = own_blocks * TILE

    def kernel(code_ref, tiles_ref, out_ref, flipped_ref, total):
        source = pl.program_id(0) + first
        for r in range(own_blocks):
            total[...] = jnp.zeros_like(total)
            for t in range(TPR):

                @pl.when(code_ref[r * TPR + t] == source)
                def _():
                    total[...] += tiles_ref[r, t].astype(F32)

            whole = total[...]
            out_ref[0, r * TILE : (r + 1) * TILE, :] = whole.astype(BF16)
            flipped_ref[0, :, r * TILE : (r + 1) * TILE] = whole.T.astype(BF16)

    return pl.pallas_call(
        kernel,
        grid=(count,),
        out_shape=[
            jax.ShapeDtypeStruct((count, rows, TILE), BF16),
            jax.ShapeDtypeStruct((count, TILE, rows), BF16),
        ],
        in_specs=[SMEM, pl.BlockSpec(tiles.shape, lambda j: (0, 0, 0, 0))],
        out_specs=[
            pl.BlockSpec((1, rows, TILE), lambda j: (j, 0, 0)),
            pl.BlockSpec((1, TILE, rows), lambda j: (j, 0, 0)),
        ],
        scratch_shapes=[pltpu.VMEM((TILE, TILE), F32)],
        compiler_params=pltpu.CompilerParams(vmem_limit_bytes=16 * 1024 * 1024),
        cost_estimate=pl.CostEstimate(
            flops=0, bytes_accessed=2 * tiles.size + 4 * count * rows * TILE, transcendentals=0
        ),
    )(code, tiles)


def early_kernel(info, matrix, own, partner, *rest):
    *direct, out = rest
    count = len(direct)
    total = mul(matrix[0], own[:TILE]) + mul(matrix[1], own[TILE:])
    for k in range(count):
        total += mul(matrix[2 + k], direct[k][...])
    out[...] = total + mul(matrix[2 + count], partner[block(info[2, count + 1]), :])


def late_kernel(info, matrix, early, inverse, *rest):
    *passed, out, away = rest
    total = early[...]
    for k, piece in enumerate(passed):
        total += mul(matrix[k], piece[...])
    out[...] = (total * inverse[...]).astype(BF16)
    away[...] = out[block(1 - info[3, 0]), :]


def slope_kernel(info, self_part, agg, agg_in, w_own, w_other, cot_own, cot_in, slope, keep, away, cot, hid):
    feat = info[3, 0]
    width = cot_own.shape[1]
    mine = pl.ds(pl.multiple_of(feat * width, width), width)
    other = pl.ds(pl.multiple_of((1 - feat) * width, width), width)
    cot[:, mine] = cot_own[...]
    cot[:, other] = cot_in[...]
    own_rows = agg[block(feat), :]
    step = 256
    for c in range(0, slope.shape[1], step):
        cols = slice(c, c + step)
        pre = self_part[:, cols] + mul(own_rows, w_own[:, cols]) + mul(agg_in[...], w_other[:, cols])
        s = jax.nn.sigmoid(pre)
        hid[:, cols] = (pre * s).astype(BF16)
        slope[:, cols] = (cot[:, cols].astype(F32) * s * (1.0 + pre * (1.0 - s))).astype(BF16)
    keep[...] = hid[:, mine]
    away[...] = hid[:, other]


def pieces_kernel(count, info, slope_own, slope_in, w_neigh, inverse, early, late, slope, scaled, partner, *outs):
    feat = info[3, 0]
    slope[block(feat), :] = slope_own[...]
    slope[block(1 - feat), :] = slope_in[...]
    scaled[...] = (mul(slope[...], w_neigh[...], COLS_BY_COLS) * inverse[...]).astype(BF16)
    for k in range(count):
        outs[k][...] = mul(late[k], scaled[...]).astype(BF16)
    for k in range(count):
        outs[count + k][...] = mul(early[2 + k], scaled[...]).astype(BF16)
    partner[...] = mul(early[2 + count], scaled[...])


def terms_kernel(info, slope, features_t, agg_t, keep_self, away_self, keep_neigh, away_neigh):
    node = info[3, 1]
    low = node % 2
    high = node // 2
    width = keep_self.shape[2]
    for left, keep, away in ((features_t, keep_self, away_self), (agg_t, keep_neigh, away_neigh)):
        for p in range(keep.shape[0]):
            both = mul(left[...], slope[:, 2 * p * width : 2 * (p + 1) * width])
            a, b = both[:, :width], both[:, width:]
            at = jnp.bitwise_xor(high, p)
            keep[at] = jnp.where(low == 0, a, b)
            away[at] = jnp.where(low == 0, b, a).astype(BF16)


def base_kernel(info, slope, w_self, scaled, early, out):
    back = mul(slope[...], w_self[...], COLS_BY_COLS)
    for b in range(2):
        rows = slice(b * TILE, (b + 1) * TILE)
        out[rows, :] = back[rows] + mul(early[b], scaled[...])


def partner_kernel(info, own, *rest):
    *passed, out, total = rest
    total[...] = jnp.zeros_like(total)
    total[block(info[2, len(passed) + 1]), :] = own[...]
    for k, piece in enumerate(passed):
        total[block(info[1, k + 1]), :] += piece[...].astype(F32)
    out[...] = total[...].astype(BF16)


def final_kernel(info, base, partner, *rest):
    *direct, out, total = rest
    total[...] = base[...] + partner[...].astype(F32)
    for k, piece in enumerate(direct):
        total[block(info[0, k + 1]), :] += piece[...].astype(F32)
    out[...] = total[...].astype(BF16)


def on_device(features, tile_list, tile_values, degree, w_self, w_neigh, cotangent):
    nodes = lax.axis_size("node")
    me = lax.axis_index("node")
    feat = lax.axis_index("feat")
    own_rows, width = features.shape
    hidden_width = w_self.shape[1]
    own_blocks = own_rows // TILE
    slots = own_blocks * TPR
    across = nodes // 2
    near = range(1, across)

    def swap(x):
        return lax.ppermute(x, "feat", [(0, 1), (1, 0)])

    def hop(x, k):
        return lax.ppermute(x, "node", [(i, i ^ k) for i in range(nodes)])

    def halves(x):
        a, b = x[:TILE], x[TILE:]
        first = feat == 0
        return jnp.where(first, a, b), jnp.where(first, b, a)

    shape = jax.ShapeDtypeStruct

    ids = jnp.arange(nodes, dtype=jnp.int32)
    everyone = tile_list.reshape(1, nodes, slots)
    at = (ids ^ me)[:, None, None]
    that = ids[None, :, None] == at
    this = ids[None, :, None] == me
    far = me ^ across
    def seen(mask):
        return jnp.any(mask, axis=(1, 2)).astype(jnp.int32)
    info = jnp.stack(
        [
            seen(that & (everyone == 2 * me + 1)),
            seen(that & (everyone == 2 * far + 1)),
            seen(this & (everyone == 2 * at + 1)),
            jnp.where(ids == 0, feat, me).astype(jnp.int32),
        ]
    )

    partner = hop(features, across)
    direct = [hop(lax.dynamic_slice_in_dim(features, info[0, k] * TILE, TILE, 0), k) for k in near]

    mine = lax.dynamic_slice_in_dim(tile_list, me * own_blocks, own_blocks, 0).reshape(slots)
    owner = mine // own_blocks
    code = jnp.where(owner == me, mine % own_blocks, 1 + (owner ^ me))
    early, early_t = combine(code, tile_values, 0, across + 2)
    late, late_t = combine(code, tile_values, across + 2, across - 1)
    inverse = (1.0 / degree.astype(F32)).reshape(own_rows, 1)

    rows_own, rows_away = halves(features)
    cot_own, cot_away = halves(cotangent)
    rows_in, cot_in = swap(rows_away), swap(cot_away)
    w_self_in, w_neigh_in = swap(w_self), swap(w_neigh)
    self_part = mul(rows_own, w_self) + mul(rows_in, w_self_in)
    features_t = features.T

    partner = after(partner, early, late, self_part, features_t)
    passed = [hop(lax.dynamic_slice_in_dim(partner, info[1, k] * TILE, TILE, 0), k) for k in near]
    tile_flops = 2 * own_rows * TILE * width
    (summed,) = local_call(
        early_kernel,
        [shape((own_rows, width), F32)],
        [info, early, features, partner, *direct],
        (across + 2) * tile_flops,
    )
    agg, agg_away = local_call(
        late_kernel,
        [shape((own_rows, width), BF16), shape((TILE, width), BF16)],
        [info, late, summed, inverse, *passed],
        across * tile_flops,
    )
    agg_in = swap(agg_away)
    agg_t = agg.T
    slope_own, hid_keep, hid_away = local_call(
        slope_kernel,
        [shape((TILE, hidden_width), BF16), shape((TILE, width), BF16), shape((TILE, width), BF16)],
        [info, self_part, agg, agg_in, w_neigh, w_neigh_in, cot_own, cot_in],
        4 * TILE * width * hidden_width,
        [pltpu.VMEM((TILE, hidden_width), BF16)] * 2,
    )
    slope_in = swap(slope_own)
    hid_in = swap(hid_away)
    hidden = jnp.where(feat == 0, jnp.concatenate([hid_keep, hid_in]), jnp.concatenate([hid_in, hid_keep]))

    count = across - 1
    piece = shape((TILE, width), BF16)
    slope, scaled, own_piece, *pieces = local_call(
        functools.partial(pieces_kernel, count),
        [shape((own_rows, hidden_width), BF16), shape((own_rows, width), BF16), shape((TILE, width), F32)]
        + [piece] * (2 * count),
        [info, slope_own, slope_in, w_neigh, inverse, early_t, late_t],
        2 * own_rows * hidden_width * width + (nodes - 1) * tile_flops,
    )
    back_passed = [hop(pieces[k - 1], k) for k in near]
    (to_partner,) = local_call(
        partner_kernel,
        [shape((own_rows, width), BF16)],
        [info, own_piece, *back_passed],
        0,
        [pltpu.VMEM((own_rows, width), F32)],
    )
    from_partner = hop(to_partner, across)
    back_direct = [hop(after(pieces[count + k - 1], to_partner), k) for k in near]

    columns = hidden_width // nodes
    if columns % 128 == 0:
        groups = nodes // 2
        keep, away = shape((groups, width, columns), F32), shape((groups, width, columns), BF16)
        terms = local_call(
            terms_kernel,
            [keep, away, keep, away],
            [info, slope, features_t, agg_t],
            4 * own_rows * width * hidden_width,
        )
        keeps, aways = list(terms[0::2]), list(terms[1::2])
        bit = 1
        while True:
            if bit == 1:
                aways = [after(x, back_passed[0]) for x in aways]
            came = [hop(x, bit) for x in aways]
            if bit == 1:
                came = [after(x, to_partner) for x in came]
            keeps = [x + y.astype(F32) for x, y in zip(keeps, came)]
            bit *= 2
            if bit == nodes:
                break
            aways = [x[1::2].astype(BF16) for x in keeps]
            keeps = [x[0::2] for x in keeps]
        grad_self, grad_neigh = keeps[0][0], keeps[1][0]
    else:
        grad_self, grad_neigh = (
            lax.psum_scatter(mul(left, slope), "node", scatter_dimension=1, tiled=True)
            for left in (features_t, agg_t)
        )

    (base,) = local_call(
        base_kernel,
        [shape((own_rows, width), F32)],
        [info, slope, w_self, scaled, early_t],
        2 * own_rows * hidden_width * width + 2 * tile_flops,
    )
    (grad_features,) = local_call(
        final_kernel,
        [shape((own_rows, width), BF16)],
        [info, base, from_partner, *back_direct],
        0,
        [pltpu.VMEM((own_rows, width), F32)],
    )
    return (hidden, grad_features, grad_self, grad_neigh)


def solution(mesh):
    return jax.shard_map(
        on_device,
        mesh=mesh,
        in_specs=(
            P(("groups", "node"), "feat"),
            P("groups", None),
            P(("groups", "node"), None, None, None),
            P(("groups", "node")),
            P("feat", None),
            P("feat", None),
            P(("groups", "node"), "feat"),
        ),
        out_specs=(
            P(("groups", "node"), "feat"),
            P(("groups", "node"), "feat"),
            P(("groups", "feat"), "node"),
            P(("groups", "feat"), "node"),
        ),
        check_vma=False,
    )
```

```python
import functools

import jax
import jax.numpy as jnp
from jax import lax
from jax.experimental import pallas as pl
from jax.experimental.pallas import tpu as pltpu
from jax.sharding import PartitionSpec as P

TILE = 256
TPR = 8
BF16, F32 = jnp.bfloat16, jnp.float32
SMEM = pl.BlockSpec(memory_space=pltpu.SMEM)
VMEM = pl.BlockSpec(memory_space=pltpu.VMEM)
HBM = pl.BlockSpec(memory_space=pltpu.HBM)
ROWS_BY_COLS = (((1,), (0,)), ((), ()))
COLS_BY_COLS = (((1,), (1,)), ((), ()))


def mul(a, b, dims=ROWS_BY_COLS):
    return lax.dot_general(a, b, dims, preferred_element_type=F32)


def block(index):
    return pl.ds(pl.multiple_of(index * TILE, TILE), TILE)


def after(x, *earlier):
    return lax.optimization_barrier((x, earlier))[0]


def local_call(kernel, outs, ins, flops, scratch=(), scalars=1, in_hbm=()):
    moved = sum(a.size * a.dtype.itemsize for a in ins)
    moved += sum(o.size * o.dtype.itemsize for o in outs)
    held = moved + 8 * 1024 * 1024
    placed = [pltpu.HBM(o.shape, o.dtype) if i in in_hbm else o for i, o in enumerate(outs)]
    return pl.pallas_call(
        kernel,
        out_shape=placed,
        in_specs=[SMEM] * scalars + [VMEM] * (len(ins) - scalars),
        out_specs=[HBM if i in in_hbm else VMEM for i in range(len(outs))],
        scratch_shapes=list(scratch),
        compiler_params=pltpu.CompilerParams(vmem_limit_bytes=held),
        cost_estimate=pl.CostEstimate(flops=flops, bytes_accessed=moved, transcendentals=0),
    )(*ins)


def combine(code, tiles, first, count):
    own_blocks = tiles.shape[0]
    rows = own_blocks * TILE

    def kernel(code_ref, tiles_ref, out_ref, flipped_ref, total):
        source = pl.program_id(0) + first
        for r in range(own_blocks):
            total[...] = jnp.zeros_like(total)
            for t in range(TPR):

                @pl.when(code_ref[r * TPR + t] == source)
                def _():
                    total[...] += tiles_ref[r, t].astype(F32)

            whole = total[...]
            out_ref[0, r * TILE : (r + 1) * TILE, :] = whole.astype(BF16)
            flipped_ref[0, :, r * TILE : (r + 1) * TILE] = whole.T.astype(BF16)

    return pl.pallas_call(
        kernel,
        grid=(count,),
        out_shape=[
            jax.ShapeDtypeStruct((count, rows, TILE), BF16),
            jax.ShapeDtypeStruct((count, TILE, rows), BF16),
        ],
        in_specs=[SMEM, pl.BlockSpec(tiles.shape, lambda j: (0, 0, 0, 0))],
        out_specs=[
            pl.BlockSpec((1, rows, TILE), lambda j: (j, 0, 0)),
            pl.BlockSpec((1, TILE, rows), lambda j: (j, 0, 0)),
        ],
        scratch_shapes=[pltpu.VMEM((TILE, TILE), F32)],
        compiler_params=pltpu.CompilerParams(vmem_limit_bytes=16 * 1024 * 1024),
        cost_estimate=pl.CostEstimate(
            flops=0, bytes_accessed=2 * tiles.size + 4 * count * rows * TILE, transcendentals=0
        ),
    )(code, tiles)


def early_kernel(info, matrix, own, partner, *rest):
    *direct, out = rest
    count = len(direct)
    total = mul(matrix[0], own[:TILE]) + mul(matrix[1], own[TILE:])
    for k in range(count):
        total += mul(matrix[2 + k], direct[k][...])
    out[...] = total + mul(matrix[2 + count], partner[block(info[2, count + 1]), :])


def late_kernel(info, matrix, early, inverse, *rest):
    *passed, out, away = rest
    total = early[...]
    for k, piece in enumerate(passed):
        total += mul(matrix[k], piece[...])
    out[...] = (total * inverse[...]).astype(BF16)
    away[...] = out[block(1 - info[3, 0]), :]


def slope_kernel(info, self_part, agg, agg_in, w_own, w_other, cot_own, cot_in, slope, keep, away, cot, hid, sems):
    feat = info[3, 0]
    width = cot_own.shape[1]
    mine = pl.ds(pl.multiple_of(feat * width, width), width)
    other = pl.ds(pl.multiple_of((1 - feat) * width, width), width)
    cot[:, mine] = cot_own[...]
    cot[:, other] = cot_in[...]
    own_rows = agg[block(feat), :]
    step = 256
    for c in range(0, slope.shape[1], step):
        cols = slice(c, c + step)
        pre = self_part[:, cols] + mul(own_rows, w_own[:, cols]) + mul(agg_in[...], w_other[:, cols])
        s = jax.nn.sigmoid(pre)
        hid[:, cols] = (pre * s).astype(BF16)
        slope[:, cols] = (cot[:, cols].astype(F32) * s * (1.0 + pre * (1.0 - s))).astype(BF16)
    copies = [
        pltpu.make_async_copy(hid.at[:, mine], keep, sems.at[0]),
        pltpu.make_async_copy(hid.at[:, other], away, sems.at[1]),
    ]
    for copy in copies:
        copy.start()
    for copy in copies:
        copy.wait()


def pieces_kernel(count, info, slope_own, slope_in, w_neigh, inverse, early, late, slope_out, scaled_out, partner_out, *rest):
    *outs, held, slope, scaled, partner, sems = rest
    feat = info[3, 0]
    slope[block(feat), :] = slope_own[...]
    slope[block(1 - feat), :] = slope_in[...]
    scaled[...] = (mul(slope[...], w_neigh[...], COLS_BY_COLS) * inverse[...]).astype(BF16)
    copies = []
    for k in range(2 * count):
        matrix = late[k] if k < count else early[2 + k - count]
        held[k] = mul(matrix, scaled[...]).astype(BF16)
        copies.append(pltpu.make_async_copy(held.at[k], outs[k], sems.at[k]))
        copies[k].start()
    partner[...] = mul(early[2 + count], scaled[...])
    for k, (source, out) in enumerate(((slope, slope_out), (scaled, scaled_out), (partner, partner_out))):
        copies.append(pltpu.make_async_copy(source, out, sems.at[2 * count + k]))
        copies[-1].start()
    for copy in copies:
        copy.wait()


def terms_kernel(info, slope, features_t, agg_t, keep_self, away_self, keep_neigh, away_neigh):
    node = info[3, 1]
    low = node % 2
    high = node // 2
    width = keep_self.shape[2]
    for left, keep, away in ((features_t, keep_self, away_self), (agg_t, keep_neigh, away_neigh)):
        for p in range(keep.shape[0]):
            both = mul(left[...], slope[:, 2 * p * width : 2 * (p + 1) * width])
            a, b = both[:, :width], both[:, width:]
            at = jnp.bitwise_xor(high, p)
            keep[at] = jnp.where(low == 0, a, b)
            away[at] = jnp.where(low == 0, b, a).astype(BF16)


def base_kernel(info, slope, w_self, scaled, early, out):
    back = mul(slope[...], w_self[...], COLS_BY_COLS)
    for b in range(2):
        rows = slice(b * TILE, (b + 1) * TILE)
        out[rows, :] = back[rows] + mul(early[b], scaled[...])


def partner_kernel(info, own, *rest):
    *passed, out, total = rest
    total[...] = jnp.zeros_like(total)
    total[block(info[2, len(passed) + 1]), :] = own[...]
    for k, piece in enumerate(passed):
        total[block(info[1, k + 1]), :] += piece[...].astype(F32)
    out[...] = total[...].astype(BF16)


def final_kernel(info, base, partner, *rest):
    *direct, out, total = rest
    total[...] = base[...] + partner[...].astype(F32)
    for k, piece in enumerate(direct):
        total[block(info[0, k + 1]), :] += piece[...].astype(F32)
    out[...] = total[...].astype(BF16)


def on_device(features, tile_list, tile_values, degree, w_self, w_neigh, cotangent):
    nodes = lax.axis_size("node")
    me = lax.axis_index("node")
    feat = lax.axis_index("feat")
    own_rows, width = features.shape
    hidden_width = w_self.shape[1]
    own_blocks = own_rows // TILE
    slots = own_blocks * TPR
    across = nodes // 2
    near = range(1, across)

    def swap(x):
        return lax.ppermute(x, "feat", [(0, 1), (1, 0)])

    def hop(x, k):
        return lax.ppermute(x, "node", [(i, i ^ k) for i in range(nodes)])

    def halves(x):
        a, b = x[:TILE], x[TILE:]
        first = feat == 0
        return jnp.where(first, a, b), jnp.where(first, b, a)

    shape = jax.ShapeDtypeStruct

    ids = jnp.arange(nodes, dtype=jnp.int32)
    everyone = tile_list.reshape(1, nodes, slots)
    at = (ids ^ me)[:, None, None]
    that = ids[None, :, None] == at
    this = ids[None, :, None] == me
    far = me ^ across
    def seen(mask):
        return jnp.any(mask, axis=(1, 2)).astype(jnp.int32)
    info = jnp.stack(
        [
            seen(that & (everyone == 2 * me + 1)),
            seen(that & (everyone == 2 * far + 1)),
            seen(this & (everyone == 2 * at + 1)),
            jnp.where(ids == 0, feat, me).astype(jnp.int32),
        ]
    )

    partner = hop(features, across)
    direct = [hop(lax.dynamic_slice_in_dim(features, info[0, k] * TILE, TILE, 0), k) for k in near]

    mine = lax.dynamic_slice_in_dim(tile_list, me * own_blocks, own_blocks, 0).reshape(slots)
    owner = mine // own_blocks
    code = jnp.where(owner == me, mine % own_blocks, 1 + (owner ^ me))
    early, early_t = combine(code, tile_values, 0, across + 2)
    late, late_t = combine(code, tile_values, across + 2, across - 1)
    inverse = (1.0 / degree.astype(F32)).reshape(own_rows, 1)

    rows_own, rows_away = halves(features)
    cot_own, cot_away = halves(cotangent)
    rows_in, cot_in = swap(rows_away), swap(cot_away)
    w_self_in, w_neigh_in = swap(w_self), swap(w_neigh)
    self_part = mul(rows_own, w_self) + mul(rows_in, w_self_in)
    features_t = features.T

    partner = after(partner, early, late, self_part, features_t)
    passed = [hop(lax.dynamic_slice_in_dim(partner, info[1, k] * TILE, TILE, 0), k) for k in near]
    tile_flops = 2 * own_rows * TILE * width
    (summed,) = local_call(
        early_kernel,
        [shape((own_rows, width), F32)],
        [info, early, features, partner, *direct],
        (across + 2) * tile_flops,
    )
    agg, agg_away = local_call(
        late_kernel,
        [shape((own_rows, width), BF16), shape((TILE, width), BF16)],
        [info, late, summed, inverse, *passed],
        across * tile_flops,
    )
    agg_in = swap(agg_away)
    agg_t = agg.T
    slope_own, hid_keep, hid_away = local_call(
        slope_kernel,
        [shape((TILE, hidden_width), BF16), shape((TILE, width), BF16), shape((TILE, width), BF16)],
        [info, self_part, agg, agg_in, w_neigh, w_neigh_in, cot_own, cot_in],
        4 * TILE * width * hidden_width,
        [pltpu.VMEM((TILE, hidden_width), BF16)] * 2 + [pltpu.SemaphoreType.DMA((2,))],
        in_hbm=(1, 2),
    )
    slope_in = swap(slope_own)

    count = across - 1
    piece = shape((TILE, width), BF16)
    slope, scaled, own_piece, *pieces = local_call(
        functools.partial(pieces_kernel, count),
        [shape((own_rows, hidden_width), BF16), shape((own_rows, width), BF16), shape((TILE, width), F32)]
        + [piece] * (2 * count),
        [info, slope_own, slope_in, w_neigh, inverse, early_t, late_t],
        2 * own_rows * hidden_width * width + (nodes - 1) * tile_flops,
        [
            pltpu.VMEM((2 * count, TILE, width), BF16),
            pltpu.VMEM((own_rows, hidden_width), BF16),
            pltpu.VMEM((own_rows, width), BF16),
            pltpu.VMEM((TILE, width), F32),
            pltpu.SemaphoreType.DMA((2 * count + 3,)),
        ],
        in_hbm=range(3 + 2 * count),
    )
    back_passed = [hop(pieces[k - 1], k) for k in near]
    (to_partner,) = local_call(
        partner_kernel,
        [shape((own_rows, width), BF16)],
        [info, own_piece, *back_passed],
        0,
        [pltpu.VMEM((own_rows, width), F32)],
    )
    from_partner = hop(to_partner, across)
    back_direct = [hop(after(pieces[count + k - 1], to_partner), k) for k in near]
    last = to_partner

    columns = hidden_width // nodes
    if columns % 128 == 0:
        groups = nodes // 2
        keep, away = shape((groups, width, columns), F32), shape((groups, width, columns), BF16)
        terms = local_call(
            terms_kernel,
            [keep, away, keep, away],
            [info, slope, features_t, agg_t],
            4 * own_rows * width * hidden_width,
        )
        keeps, aways = list(terms[0::2]), list(terms[1::2])
        flying = [hop(after(x, *back_passed), 1) for x in aways]
        gate = to_partner
        bit = 1
        while bit < nodes:
            for i in range(2):
                keeps[i] = keeps[i] + after(flying[i], gate).astype(F32)
                if bit * 2 < nodes:
                    flying[i] = hop(keeps[i][1::2].astype(BF16), bit * 2)
                    keeps[i] = keeps[i][0::2]
                    gate = (flying[0], from_partner, *back_direct[1:])
            if bit == 1:
                last = keeps[1]
            bit *= 2
        grad_self, grad_neigh = keeps[0][0], keeps[1][0]
    else:
        grad_self, grad_neigh = (
            lax.psum_scatter(mul(left, slope), "node", scatter_dimension=1, tiled=True)
            for left in (features_t, agg_t)
        )

    hid_in = swap(after(hid_away, last))
    hidden = jnp.where(feat == 0, jnp.concatenate([hid_keep, hid_in]), jnp.concatenate([hid_in, hid_keep]))

    (base,) = local_call(
        base_kernel,
        [shape((own_rows, width), F32)],
        [info, slope, w_self, scaled, early_t],
        2 * own_rows * hidden_width * width + 2 * tile_flops,
    )
    (grad_features,) = local_call(
        final_kernel,
        [shape((own_rows, width), BF16)],
        [info, base, from_partner, *back_direct],
        0,
        [pltpu.VMEM((own_rows, width), F32)],
    )
    return (hidden, grad_features, grad_self, grad_neigh)


def solution(mesh):
    return jax.shard_map(
        on_device,
        mesh=mesh,
        in_specs=(
            P(("groups", "node"), "feat"),
            P("groups", None),
            P(("groups", "node"), None, None, None),
            P(("groups", "node")),
            P("feat", None),
            P("feat", None),
            P(("groups", "node"), "feat"),
        ),
        out_specs=(
            P(("groups", "node"), "feat"),
            P(("groups", "node"), "feat"),
            P(("groups", "feat"), "node"),
            P(("groups", "feat"), "node"),
        ),
        check_vma=False,
    )
```

```python
import functools

import jax
import jax.numpy as jnp
from jax import lax
from jax.experimental import pallas as pl
from jax.experimental.pallas import tpu as pltpu
from jax.sharding import PartitionSpec as P

TILE = 256
TPR = 8
BF16, F32 = jnp.bfloat16, jnp.float32
SMEM = pl.BlockSpec(memory_space=pltpu.SMEM)
VMEM = pl.BlockSpec(memory_space=pltpu.VMEM)
HBM = pl.BlockSpec(memory_space=pltpu.HBM)
ROWS_BY_COLS = (((1,), (0,)), ((), ()))
COLS_BY_COLS = (((1,), (1,)), ((), ()))


def mul(a, b, dims=ROWS_BY_COLS):
    return lax.dot_general(a, b, dims, preferred_element_type=F32)


def block(index):
    return pl.ds(pl.multiple_of(index * TILE, TILE), TILE)


def after(x, *earlier):
    return lax.optimization_barrier((x, earlier))[0]


def local_call(kernel, outs, ins, flops, scratch=(), scalars=1, in_hbm=()):
    moved = sum(a.size * a.dtype.itemsize for a in ins)
    moved += sum(o.size * o.dtype.itemsize for o in outs)
    held = moved + 8 * 1024 * 1024
    placed = [pltpu.HBM(o.shape, o.dtype) if i in in_hbm else o for i, o in enumerate(outs)]
    return pl.pallas_call(
        kernel,
        out_shape=placed,
        in_specs=[SMEM] * scalars + [VMEM] * (len(ins) - scalars),
        out_specs=[HBM if i in in_hbm else VMEM for i in range(len(outs))],
        scratch_shapes=list(scratch),
        compiler_params=pltpu.CompilerParams(vmem_limit_bytes=held),
        cost_estimate=pl.CostEstimate(flops=flops, bytes_accessed=moved, transcendentals=0),
    )(*ins)


def combine(code, tiles, first, count):
    own_blocks = tiles.shape[0]
    rows = own_blocks * TILE

    def kernel(code_ref, tiles_ref, out_ref, flipped_ref, total):
        source = pl.program_id(0) + first
        for r in range(own_blocks):
            total[...] = jnp.zeros_like(total)
            for t in range(TPR):

                @pl.when(code_ref[r * TPR + t] == source)
                def _():
                    total[...] += tiles_ref[r, t].astype(F32)

            whole = total[...]
            out_ref[0, r * TILE : (r + 1) * TILE, :] = whole.astype(BF16)
            flipped_ref[0, :, r * TILE : (r + 1) * TILE] = whole.T.astype(BF16)

    return pl.pallas_call(
        kernel,
        grid=(count,),
        out_shape=[
            jax.ShapeDtypeStruct((count, rows, TILE), BF16),
            jax.ShapeDtypeStruct((count, TILE, rows), BF16),
        ],
        in_specs=[SMEM, pl.BlockSpec(tiles.shape, lambda j: (0, 0, 0, 0))],
        out_specs=[
            pl.BlockSpec((1, rows, TILE), lambda j: (j, 0, 0)),
            pl.BlockSpec((1, TILE, rows), lambda j: (j, 0, 0)),
        ],
        scratch_shapes=[pltpu.VMEM((TILE, TILE), F32)],
        compiler_params=pltpu.CompilerParams(vmem_limit_bytes=16 * 1024 * 1024),
        cost_estimate=pl.CostEstimate(
            flops=0, bytes_accessed=2 * tiles.size + 4 * count * rows * TILE, transcendentals=0
        ),
    )(code, tiles)


def early_kernel(info, matrix, own, partner, *rest):
    *direct, out = rest
    count = len(direct)
    total = mul(matrix[0], own[:TILE]) + mul(matrix[1], own[TILE:])
    for k in range(count):
        total += mul(matrix[2 + k], direct[k][...])
    out[...] = total + mul(matrix[2 + count], partner[block(info[2, count + 1]), :])


def late_kernel(info, matrix, early, inverse, *rest):
    *passed, out, away = rest
    total = early[...]
    for k, piece in enumerate(passed):
        total += mul(matrix[k], piece[...])
    out[...] = (total * inverse[...]).astype(BF16)
    away[...] = out[block(1 - info[3, 0]), :]


def slope_kernel(info, self_part, agg, agg_in, w_own, w_other, cot_own, cot_in, slope, halves, cot, hid, sems):
    feat = info[3, 0]
    width = cot_own.shape[1]
    mine = pl.ds(pl.multiple_of(feat * width, width), width)
    other = pl.ds(pl.multiple_of((1 - feat) * width, width), width)
    cot[:, mine] = cot_own[...]
    cot[:, other] = cot_in[...]
    own_rows = agg[block(feat), :]
    step = 256
    copies = []
    for c in range(0, slope.shape[1], step):
        cols = slice(c, c + step)
        pre = self_part[:, cols] + mul(own_rows, w_own[:, cols]) + mul(agg_in[...], w_other[:, cols])
        s = jax.nn.sigmoid(pre)
        hid[:, cols] = (pre * s).astype(BF16)
        slope[:, cols] = (cot[:, cols].astype(F32) * s * (1.0 + pre * (1.0 - s))).astype(BF16)
        if (c + step) % width == 0:
            half = c // width
            source = hid.at[:, half * width : (half + 1) * width]
            copies.append(pltpu.make_async_copy(source, halves.at[jnp.bitwise_xor(half, feat)], sems.at[half]))
            copies[-1].start()
    for copy in copies:
        copy.wait()


def pieces_kernel(count, info, slope_own, slope_in, w_neigh, inverse, early, late, slope_out, scaled_out, partner_out, *rest):
    *outs, held, slope, scaled, partner, sems = rest
    feat = info[3, 0]
    copies = []

    def send(source, out):
        copies.append(pltpu.make_async_copy(source, out, sems.at[len(copies)]))
        copies[-1].start()

    slope[block(feat), :] = slope_own[...]
    slope[block(1 - feat), :] = slope_in[...]
    send(slope, slope_out)
    scaled[...] = (mul(slope[...], w_neigh[...], COLS_BY_COLS) * inverse[...]).astype(BF16)
    send(scaled, scaled_out)
    partner[...] = mul(early[2 + count], scaled[...])
    send(partner, partner_out)
    for k in range(2 * count):
        matrix = late[k] if k < count else early[2 + k - count]
        held[k] = mul(matrix, scaled[...]).astype(BF16)
        send(held.at[k], outs[k])
    for copy in copies:
        copy.wait()


def terms_kernel(info, slope, features_t, agg_t, keep_self, away_self, keep_neigh, away_neigh):
    node = info[3, 1]
    low = node % 2
    high = node // 2
    width = keep_self.shape[2]
    for left, keep, away in ((features_t, keep_self, away_self), (agg_t, keep_neigh, away_neigh)):
        for p in range(keep.shape[0]):
            both = mul(left[...], slope[:, 2 * p * width : 2 * (p + 1) * width])
            a, b = both[:, :width], both[:, width:]
            at = jnp.bitwise_xor(high, p)
            keep[at] = jnp.where(low == 0, a, b)
            away[at] = jnp.where(low == 0, b, a).astype(BF16)


def base_kernel(info, slope, w_self, scaled, early, out):
    back = mul(slope[...], w_self[...], COLS_BY_COLS)
    for b in range(2):
        rows = slice(b * TILE, (b + 1) * TILE)
        out[rows, :] = back[rows] + mul(early[b], scaled[...])


def partner_kernel(info, own, *rest):
    *passed, out, total = rest
    total[...] = jnp.zeros_like(total)
    total[block(info[2, len(passed) + 1]), :] = own[...]
    for k, piece in enumerate(passed):
        total[block(info[1, k + 1]), :] += piece[...].astype(F32)
    out[...] = total[...].astype(BF16)


def final_kernel(info, base, partner, *rest):
    *direct, out, total = rest
    total[...] = base[...] + partner[...].astype(F32)
    for k, piece in enumerate(direct):
        total[block(info[0, k + 1]), :] += piece[...].astype(F32)
    out[...] = total[...].astype(BF16)


def on_device(features, tile_list, tile_values, degree, w_self, w_neigh, cotangent):
    nodes = lax.axis_size("node")
    me = lax.axis_index("node")
    feat = lax.axis_index("feat")
    own_rows, width = features.shape
    hidden_width = w_self.shape[1]
    own_blocks = own_rows // TILE
    slots = own_blocks * TPR
    across = nodes // 2
    near = range(1, across)

    def swap(x):
        return lax.ppermute(x, "feat", [(0, 1), (1, 0)])

    def hop(x, k):
        return lax.ppermute(x, "node", [(i, i ^ k) for i in range(nodes)])

    def halves(x):
        a, b = x[:TILE], x[TILE:]
        first = feat == 0
        return jnp.where(first, a, b), jnp.where(first, b, a)

    shape = jax.ShapeDtypeStruct

    ids = jnp.arange(nodes, dtype=jnp.int32)
    everyone = tile_list.reshape(1, nodes, slots)
    at = (ids ^ me)[:, None, None]
    that = ids[None, :, None] == at
    this = ids[None, :, None] == me
    far = me ^ across
    def seen(mask):
        return jnp.any(mask, axis=(1, 2)).astype(jnp.int32)
    info = jnp.stack(
        [
            seen(that & (everyone == 2 * me + 1)),
            seen(that & (everyone == 2 * far + 1)),
            seen(this & (everyone == 2 * at + 1)),
            jnp.where(ids == 0, feat, me).astype(jnp.int32),
        ]
    )

    partner = hop(features, across)
    direct = [hop(lax.dynamic_slice_in_dim(features, info[0, k] * TILE, TILE, 0), k) for k in near]

    mine = lax.dynamic_slice_in_dim(tile_list, me * own_blocks, own_blocks, 0).reshape(slots)
    owner = mine // own_blocks
    code = jnp.where(owner == me, mine % own_blocks, 1 + (owner ^ me))
    early, early_t = combine(code, tile_values, 0, across + 2)
    late, late_t = combine(code, tile_values, across + 2, across - 1)
    inverse = (1.0 / degree.astype(F32)).reshape(own_rows, 1)

    rows_own, rows_away = halves(features)
    cot_own, cot_away = halves(cotangent)
    rows_in, cot_in = swap(rows_away), swap(cot_away)
    w_self_in, w_neigh_in = swap(w_self), swap(w_neigh)
    self_part = mul(rows_own, w_self) + mul(rows_in, w_self_in)
    features_t = features.T

    partner = after(partner, early, late, self_part, features_t)
    passed = [hop(lax.dynamic_slice_in_dim(partner, info[1, k] * TILE, TILE, 0), k) for k in near]
    tile_flops = 2 * own_rows * TILE * width
    (summed,) = local_call(
        early_kernel,
        [shape((own_rows, width), F32)],
        [info, early, features, partner, *direct],
        (across + 2) * tile_flops,
    )
    agg, agg_away = local_call(
        late_kernel,
        [shape((own_rows, width), BF16), shape((TILE, width), BF16)],
        [info, late, summed, inverse, *passed],
        across * tile_flops,
    )
    agg_in = swap(agg_away)
    agg_t = agg.T
    slope_own, hid_halves = local_call(
        slope_kernel,
        [shape((TILE, hidden_width), BF16), shape((2, TILE, width), BF16)],
        [info, self_part, agg, agg_in, w_neigh, w_neigh_in, cot_own, cot_in],
        4 * TILE * width * hidden_width,
        [pltpu.VMEM((TILE, hidden_width), BF16)] * 2 + [pltpu.SemaphoreType.DMA((2,))],
        in_hbm=(1,),
    )
    slope_in = swap(slope_own)

    count = across - 1
    piece = shape((TILE, width), BF16)
    slope, scaled, own_piece, *pieces = local_call(
        functools.partial(pieces_kernel, count),
        [shape((own_rows, hidden_width), BF16), shape((own_rows, width), BF16), shape((TILE, width), F32)]
        + [piece] * (2 * count),
        [info, slope_own, slope_in, w_neigh, inverse, early_t, late_t],
        2 * own_rows * hidden_width * width + (nodes - 1) * tile_flops,
        [
            pltpu.VMEM((2 * count, TILE, width), BF16),
            pltpu.VMEM((own_rows, hidden_width), BF16),
            pltpu.VMEM((own_rows, width), BF16),
            pltpu.VMEM((TILE, width), F32),
            pltpu.SemaphoreType.DMA((2 * count + 3,)),
        ],
        in_hbm=range(3 + 2 * count),
    )
    back_passed = [hop(pieces[k - 1], k) for k in near]
    (to_partner,) = local_call(
        partner_kernel,
        [shape((own_rows, width), BF16)],
        [info, own_piece, *back_passed],
        0,
        [pltpu.VMEM((own_rows, width), F32)],
    )
    from_partner = hop(to_partner, across)
    back_direct = [hop(after(pieces[count + k - 1], to_partner), k) for k in near]
    last = to_partner

    columns = hidden_width // nodes
    if columns % 128 == 0:
        groups = nodes // 2
        keep, away = shape((groups, width, columns), F32), shape((groups, width, columns), BF16)
        terms = local_call(
            terms_kernel,
            [keep, away, keep, away],
            [info, slope, features_t, agg_t],
            4 * own_rows * width * hidden_width,
        )
        keeps, aways = list(terms[0::2]), list(terms[1::2])
        flying = [hop(after(x, *back_passed), 1) for x in aways]
        gate = to_partner
        bit = 1
        while bit < nodes:
            for i in range(2):
                keeps[i] = keeps[i] + after(flying[i], gate).astype(F32)
                if bit * 2 < nodes:
                    flying[i] = hop(keeps[i][1::2].astype(BF16), bit * 2)
                    keeps[i] = keeps[i][0::2]
                    gate = (flying[0], from_partner, *back_direct[1:])
            if bit == 1:
                last = keeps[1]
            bit *= 2
        grad_self, grad_neigh = keeps[0][0], keeps[1][0]
    else:
        grad_self, grad_neigh = (
            lax.psum_scatter(mul(left, slope), "node", scatter_dimension=1, tiled=True)
            for left in (features_t, agg_t)
        )

    hid_keep, hid_in = hid_halves[0], swap(after(hid_halves[1], last))
    hidden = jnp.where(feat == 0, jnp.concatenate([hid_keep, hid_in]), jnp.concatenate([hid_in, hid_keep]))

    (base,) = local_call(
        base_kernel,
        [shape((own_rows, width), F32)],
        [info, slope, w_self, scaled, early_t],
        2 * own_rows * hidden_width * width + 2 * tile_flops,
    )
    (grad_features,) = local_call(
        final_kernel,
        [shape((own_rows, width), BF16)],
        [info, base, from_partner, *back_direct],
        0,
        [pltpu.VMEM((own_rows, width), F32)],
    )
    return (hidden, grad_features, grad_self, grad_neigh)


def solution(mesh):
    return jax.shard_map(
        on_device,
        mesh=mesh,
        in_specs=(
            P(("groups", "node"), "feat"),
            P("groups", None),
            P(("groups", "node"), None, None, None),
            P(("groups", "node")),
            P("feat", None),
            P("feat", None),
            P(("groups", "node"), "feat"),
        ),
        out_specs=(
            P(("groups", "node"), "feat"),
            P(("groups", "node"), "feat"),
            P(("groups", "feat"), "node"),
            P(("groups", "feat"), "node"),
        ),
        check_vma=False,
    )
```

```python
import functools

import jax
import jax.numpy as jnp
from jax import lax
from jax.experimental import pallas as pl
from jax.experimental.pallas import tpu as pltpu
from jax.sharding import PartitionSpec as P

TILE = 256
TPR = 8
BF16, F32 = jnp.bfloat16, jnp.float32
SMEM = pl.BlockSpec(memory_space=pltpu.SMEM)
VMEM = pl.BlockSpec(memory_space=pltpu.VMEM)
HBM = pl.BlockSpec(memory_space=pltpu.HBM)
ROWS_BY_COLS = (((1,), (0,)), ((), ()))
COLS_BY_COLS = (((1,), (1,)), ((), ()))


def mul(a, b, dims=ROWS_BY_COLS):
    return lax.dot_general(a, b, dims, preferred_element_type=F32)


def block(index):
    return pl.ds(pl.multiple_of(index * TILE, TILE), TILE)


def after(x, *earlier):
    return lax.optimization_barrier((x, earlier))[0]


def local_call(kernel, outs, ins, flops, scratch=(), scalars=1, in_hbm=()):
    moved = sum(a.size * a.dtype.itemsize for a in ins)
    moved += sum(o.size * o.dtype.itemsize for o in outs)
    held = moved + 8 * 1024 * 1024
    placed = [pltpu.HBM(o.shape, o.dtype) if i in in_hbm else o for i, o in enumerate(outs)]
    return pl.pallas_call(
        kernel,
        out_shape=placed,
        in_specs=[SMEM] * scalars + [VMEM] * (len(ins) - scalars),
        out_specs=[HBM if i in in_hbm else VMEM for i in range(len(outs))],
        scratch_shapes=list(scratch),
        compiler_params=pltpu.CompilerParams(vmem_limit_bytes=held),
        cost_estimate=pl.CostEstimate(flops=flops, bytes_accessed=moved, transcendentals=0),
    )(*ins)


def combine(code, tiles, first, count):
    own_blocks = tiles.shape[0]
    rows = own_blocks * TILE

    def kernel(code_ref, tiles_ref, out_ref, flipped_ref, total):
        source = pl.program_id(0) + first
        for r in range(own_blocks):
            total[...] = jnp.zeros_like(total)
            for t in range(TPR):

                @pl.when(code_ref[r * TPR + t] == source)
                def _():
                    total[...] += tiles_ref[r, t].astype(F32)

            whole = total[...]
            out_ref[0, r * TILE : (r + 1) * TILE, :] = whole.astype(BF16)
            flipped_ref[0, :, r * TILE : (r + 1) * TILE] = whole.T.astype(BF16)

    return pl.pallas_call(
        kernel,
        grid=(count,),
        out_shape=[
            jax.ShapeDtypeStruct((count, rows, TILE), BF16),
            jax.ShapeDtypeStruct((count, TILE, rows), BF16),
        ],
        in_specs=[SMEM, pl.BlockSpec(tiles.shape, lambda j: (0, 0, 0, 0))],
        out_specs=[
            pl.BlockSpec((1, rows, TILE), lambda j: (j, 0, 0)),
            pl.BlockSpec((1, TILE, rows), lambda j: (j, 0, 0)),
        ],
        scratch_shapes=[pltpu.VMEM((TILE, TILE), F32)],
        compiler_params=pltpu.CompilerParams(vmem_limit_bytes=16 * 1024 * 1024),
        cost_estimate=pl.CostEstimate(
            flops=0, bytes_accessed=2 * tiles.size + 4 * count * rows * TILE, transcendentals=0
        ),
    )(code, tiles)


def early_kernel(info, matrix, own, partner, *rest):
    *direct, out = rest
    count = len(direct)
    total = mul(matrix[0], own[:TILE]) + mul(matrix[1], own[TILE:])
    for k in range(count):
        total += mul(matrix[2 + k], direct[k][...])
    out[...] = total + mul(matrix[2 + count], partner[block(info[2, count + 1]), :])


def late_kernel(info, matrix, early, inverse, *rest):
    *passed, out, away = rest
    total = early[...]
    for k, piece in enumerate(passed):
        total += mul(matrix[k], piece[...])
    out[...] = (total * inverse[...]).astype(BF16)
    away[...] = out[block(1 - info[3, 0]), :]


def slope_kernel(info, self_part, agg, agg_in, w_own, w_other, cot_own, cot_in, slope, halves, cot, hid, sems):
    feat = info[3, 0]
    width = cot_own.shape[1]
    mine = pl.ds(pl.multiple_of(feat * width, width), width)
    other = pl.ds(pl.multiple_of((1 - feat) * width, width), width)
    cot[:, mine] = cot_own[...]
    cot[:, other] = cot_in[...]
    own_rows = agg[block(feat), :]
    step = 256
    copies = []
    for c in range(0, slope.shape[1], step):
        cols = slice(c, c + step)
        pre = self_part[:, cols] + mul(own_rows, w_own[:, cols]) + mul(agg_in[...], w_other[:, cols])
        s = jax.nn.sigmoid(pre)
        hid[:, cols] = (pre * s).astype(BF16)
        slope[:, cols] = (cot[:, cols].astype(F32) * s * (1.0 + pre * (1.0 - s))).astype(BF16)
        if (c + step) % width == 0:
            half = c // width
            source = hid.at[:, half * width : (half + 1) * width]
            copies.append(pltpu.make_async_copy(source, halves.at[jnp.bitwise_xor(half, feat)], sems.at[half]))
            copies[-1].start()
    for copy in copies:
        copy.wait()


def pieces_kernel(count, info, slope_own, slope_in, w_neigh, inverse, early, late, slope_out, scaled_out, partner_out, *rest):
    *outs, held, slope, scaled, partner, sems = rest
    feat = info[3, 0]
    copies = []

    def send(source, out):
        copies.append(pltpu.make_async_copy(source, out, sems.at[len(copies)]))
        copies[-1].start()

    slope[block(feat), :] = slope_own[...]
    slope[block(1 - feat), :] = slope_in[...]
    send(slope, slope_out)
    scaled[...] = (mul(slope[...], w_neigh[...], COLS_BY_COLS) * inverse[...]).astype(BF16)
    send(scaled, scaled_out)
    partner[...] = mul(early[2 + count], scaled[...])
    send(partner, partner_out)
    for k in range(2 * count):
        matrix = late[k] if k < count else early[2 + k - count]
        held[k] = mul(matrix, scaled[...]).astype(BF16)
        send(held.at[k], outs[k])
    for copy in copies:
        copy.wait()


def terms_kernel(info, slope, features_t, agg_t, keep_self, away_self, keep_neigh, away_neigh):
    node = info[3, 1]
    low = node % 2
    high = node // 2
    width = keep_self.shape[2]
    for left, keep, away in ((features_t, keep_self, away_self), (agg_t, keep_neigh, away_neigh)):
        for p in range(keep.shape[0]):
            both = mul(left[...], slope[:, 2 * p * width : 2 * (p + 1) * width])
            a, b = both[:, :width], both[:, width:]
            at = jnp.bitwise_xor(high, p)
            keep[at] = jnp.where(low == 0, a, b)
            away[at] = jnp.where(low == 0, b, a).astype(BF16)


def base_kernel(info, slope, w_self, scaled, early, out):
    back = mul(slope[...], w_self[...], COLS_BY_COLS)
    for b in range(2):
        rows = slice(b * TILE, (b + 1) * TILE)
        out[rows, :] = back[rows] + mul(early[b], scaled[...])


def partner_kernel(info, own, *rest):
    *passed, out, total = rest
    total[...] = jnp.zeros_like(total)
    total[block(info[2, len(passed) + 1]), :] = own[...]
    for k, piece in enumerate(passed):
        total[block(info[1, k + 1]), :] += piece[...].astype(F32)
    out[...] = total[...].astype(BF16)


def final_kernel(info, base, partner, *rest):
    *direct, out, total = rest
    total[...] = base[...] + partner[...].astype(F32)
    for k, piece in enumerate(direct):
        total[block(info[0, k + 1]), :] += piece[...].astype(F32)
    out[...] = total[...].astype(BF16)


def on_device(features, tile_list, tile_values, degree, w_self, w_neigh, cotangent):
    nodes = lax.axis_size("node")
    me = lax.axis_index("node")
    feat = lax.axis_index("feat")
    own_rows, width = features.shape
    hidden_width = w_self.shape[1]
    own_blocks = own_rows // TILE
    slots = own_blocks * TPR
    across = nodes // 2
    near = range(1, across)

    def swap(x):
        return lax.ppermute(x, "feat", [(0, 1), (1, 0)])

    def hop(x, k):
        return lax.ppermute(x, "node", [(i, i ^ k) for i in range(nodes)])

    def halves(x):
        a, b = x[:TILE], x[TILE:]
        first = feat == 0
        return jnp.where(first, a, b), jnp.where(first, b, a)

    shape = jax.ShapeDtypeStruct

    ids = jnp.arange(nodes, dtype=jnp.int32)
    everyone = tile_list.reshape(1, nodes, slots)
    at = (ids ^ me)[:, None, None]
    that = ids[None, :, None] == at
    this = ids[None, :, None] == me
    far = me ^ across
    def seen(mask):
        return jnp.any(mask, axis=(1, 2)).astype(jnp.int32)
    info = jnp.stack(
        [
            seen(that & (everyone == 2 * me + 1)),
            seen(that & (everyone == 2 * far + 1)),
            seen(this & (everyone == 2 * at + 1)),
            jnp.where(ids == 0, feat, me).astype(jnp.int32),
        ]
    )

    partner = hop(features, across)
    rows_own, rows_away = halves(features)
    rows_in, w_self_in = swap(rows_away), swap(w_self)
    picked = [lax.dynamic_slice_in_dim(features, info[0, k] * TILE, TILE, 0) for k in near]
    direct = [hop(x, k) for x, k in zip(picked, near)]

    mine = lax.dynamic_slice_in_dim(tile_list, me * own_blocks, own_blocks, 0).reshape(slots)
    owner = mine // own_blocks
    code = jnp.where(owner == me, mine % own_blocks, 1 + (owner ^ me))
    code = after(code, rows_in, w_self_in)
    early, early_t = combine(code, tile_values, 0, across + 2)
    late, late_t = combine(code, tile_values, across + 2, across - 1)
    inverse = (1.0 / degree.astype(F32)).reshape(own_rows, 1)

    cot_own, cot_away = halves(cotangent)
    cot_in, w_neigh_in = swap(cot_away), swap(w_neigh)
    self_part = mul(rows_own, w_self) + mul(rows_in, w_self_in)
    features_t = features.T

    partner = after(partner, early, late, self_part, features_t)
    passed = [hop(lax.dynamic_slice_in_dim(partner, info[1, k] * TILE, TILE, 0), k) for k in near]
    tile_flops = 2 * own_rows * TILE * width
    (summed,) = local_call(
        early_kernel,
        [shape((own_rows, width), F32)],
        [info, early, features, partner, *direct],
        (across + 2) * tile_flops,
    )
    agg, agg_away = local_call(
        late_kernel,
        [shape((own_rows, width), BF16), shape((TILE, width), BF16)],
        [info, late, summed, inverse, *passed],
        across * tile_flops,
    )
    agg_in = swap(agg_away)
    agg_t = agg.T
    slope_own, hid_halves = local_call(
        slope_kernel,
        [shape((TILE, hidden_width), BF16), shape((2, TILE, width), BF16)],
        [info, self_part, agg, agg_in, w_neigh, w_neigh_in, cot_own, cot_in],
        4 * TILE * width * hidden_width,
        [pltpu.VMEM((TILE, hidden_width), BF16)] * 2 + [pltpu.SemaphoreType.DMA((2,))],
        in_hbm=(1,),
    )
    slope_in = swap(slope_own)

    count = across - 1
    piece = shape((TILE, width), BF16)
    slope, scaled, own_piece, *pieces = local_call(
        functools.partial(pieces_kernel, count),
        [shape((own_rows, hidden_width), BF16), shape((own_rows, width), BF16), shape((TILE, width), F32)]
        + [piece] * (2 * count),
        [info, slope_own, slope_in, w_neigh, inverse, early_t, late_t],
        2 * own_rows * hidden_width * width + (nodes - 1) * tile_flops,
        [
            pltpu.VMEM((2 * count, TILE, width), BF16),
            pltpu.VMEM((own_rows, hidden_width), BF16),
            pltpu.VMEM((own_rows, width), BF16),
            pltpu.VMEM((TILE, width), F32),
            pltpu.SemaphoreType.DMA((2 * count + 3,)),
        ],
        in_hbm=range(3 + 2 * count),
    )
    back_passed = [hop(pieces[k - 1], k) for k in near]
    (to_partner,) = local_call(
        partner_kernel,
        [shape((own_rows, width), BF16)],
        [info, own_piece, *back_passed],
        0,
        [pltpu.VMEM((own_rows, width), F32)],
    )
    from_partner = hop(to_partner, across)
    back_direct = [hop(after(pieces[count + k - 1], to_partner), k) for k in near]
    last = to_partner

    columns = hidden_width // nodes
    if columns % 128 == 0:
        groups = nodes // 2
        keep, away = shape((groups, width, columns), F32), shape((groups, width, columns), BF16)
        terms = local_call(
            terms_kernel,
            [keep, away, keep, away],
            [info, slope, features_t, agg_t],
            4 * own_rows * width * hidden_width,
        )
        keeps, aways = list(terms[0::2]), list(terms[1::2])
        flying = [hop(after(x, *back_passed), 1) for x in aways]
        gate = to_partner
        bit = 1
        while bit < nodes:
            for i in range(2):
                keeps[i] = keeps[i] + after(flying[i], gate).astype(F32)
                if bit * 2 < nodes:
                    flying[i] = hop(keeps[i][1::2].astype(BF16), bit * 2)
                    keeps[i] = keeps[i][0::2]
                    gate = (flying[0], from_partner, *back_direct[1:])
            if bit == 1:
                last = keeps[1]
            bit *= 2
        grad_self, grad_neigh = keeps[0][0], keeps[1][0]
    else:
        grad_self, grad_neigh = (
            lax.psum_scatter(mul(left, slope), "node", scatter_dimension=1, tiled=True)
            for left in (features_t, agg_t)
        )

    hid_keep, hid_in = hid_halves[0], swap(after(hid_halves[1], last))
    hidden = jnp.where(feat == 0, jnp.concatenate([hid_keep, hid_in]), jnp.concatenate([hid_in, hid_keep]))

    (base,) = local_call(
        base_kernel,
        [shape((own_rows, width), F32)],
        [info, slope, w_self, scaled, early_t],
        2 * own_rows * hidden_width * width + 2 * tile_flops,
    )
    (grad_features,) = local_call(
        final_kernel,
        [shape((own_rows, width), BF16)],
        [info, base, from_partner, *back_direct],
        0,
        [pltpu.VMEM((own_rows, width), F32)],
    )
    return (hidden, grad_features, grad_self, grad_neigh)


def solution(mesh):
    return jax.shard_map(
        on_device,
        mesh=mesh,
        in_specs=(
            P(("groups", "node"), "feat"),
            P("groups", None),
            P(("groups", "node"), None, None, None),
            P(("groups", "node")),
            P("feat", None),
            P("feat", None),
            P(("groups", "node"), "feat"),
        ),
        out_specs=(
            P(("groups", "node"), "feat"),
            P(("groups", "node"), "feat"),
            P(("groups", "feat"), "node"),
            P(("groups", "feat"), "node"),
        ),
        check_vma=False,
    )
```
